32 devices in a mesh: req: 2 (over x), blk: 16 (over z, y, core).
Axes of the slice: x: 2, y: 2, z: 4, core: 2. Of those that a mesh axis runs over, the one named last changes fastest.
Arguments:
- tokens: bfloat16 [32, 128, 1536], P(('req', 'blk')), may hold values from -6 to 6
- cache_kv: bfloat16 [32, 2, 256, 384], P(('req', 'blk')), may hold values from -200 to 200
- cache_len: int32 [32], P(('req', 'blk')), may hold values from 2 to 256, as said below
- holder: int32 [32], P(('req', 'blk')), may hold values from 0 to 1, as said below
- accept: int32 [32, 128], P(('req', 'blk')), may hold values from 0 to 1, as said below
- attn_gain: float32 [1536], replicated, may hold values from 0.1 to 1.9
- q_weight: bfloat16 [1536, 768], replicated, may hold values from -0.15625 to 0.15625
- k_weight: bfloat16 [1536, 384], replicated, may hold values from -0.15625 to 0.15625
- v_weight: bfloat16 [1536, 384], replicated, may hold values from -0.15625 to 0.15625
- o_weight: bfloat16 [768, 1536], replicated, may hold values from -0.21875 to 0.21875
- ffn_gain: float32 [1536], replicated, may hold values from 0.4 to 2.5
- w_gate: bfloat16 [1536, 4096], P(None, 'blk'), may hold values from -0.15625 to 0.15625
- w_up: bfloat16 [1536, 4096], P(None, 'blk'), may hold values from -0.15625 to 0.15625
- w_down: bfloat16 [4096, 1536], P('blk'), may hold values from -0.09375 to 0.09375
Outputs:
- refined: float32 [32, 128, 1536], P(('req', 'blk'))
The draws below stay inside these ranges and needn't reach their ends.
Inputs may be any that keep to these rules, and one draw needn't show every extreme that they name: `holder`: requests whose numbers agree modulo 16 have distinct holders. `cache_len`: some request has exactly 256 cached positions. `accept`: each request accepts exactly 64 positions.
All inputs are finite; a program needn't handle non-finite values.
Results may differ from the reference program's by a relative error of at most 0.04.
Values may be sent and summed in bfloat16 or wider, within the bound.
A program may use at most 128 MiB of HBM per device.

```python
import math
import jax
import jax.numpy as jnp
from jax import lax

D = 1536
HEADS = 8
KV_HEADS = 4
HEAD = 96
FF = 4096
BLOCK = 128
ACCEPT = 64
CSLOT = 256
QW = 768
KVW = 384
REQ_GROUP = 2
BLK_GROUP = 16
FF_DEV = 256
REQUESTS = 32


def draw_cache_len(key, part):
    first_key, second_key = jax.random.split(key)
    lengths = jax.random.randint(first_key, (REQUESTS,), 2, CSLOT + 1)
    longest = jax.random.randint(second_key, (), 0, REQUESTS)
    return jnp.where(jnp.arange(REQUESTS) == longest, CSLOT, lengths).astype(jnp.int32)


def draw_holder(key, part):
    column_keys = jax.random.split(key, BLK_GROUP)

    def column(column_key):
        return jax.random.permutation(column_key, REQ_GROUP).astype(jnp.int32)
    columns = jax.vmap(column)(column_keys)
    return columns.T.reshape(REQUESTS).astype(jnp.int32)


def draw_accept(key, part):
    row_keys = jax.random.split(key, REQUESTS)

    def one_row(row_key):
        order = jax.random.permutation(row_key, BLOCK)
        return jnp.zeros((BLOCK,), jnp.int32).at[order[:ACCEPT]].set(1)
    return jax.vmap(one_row)(row_keys).astype(jnp.int32)


def draw_cache_kv(key, part):
    base_key = jax.random.fold_in(key, 0)
    shape = (REQUESTS, 2, CSLOT, KVW)
    drawn = jnp.clip(jax.random.normal(base_key, shape, jnp.float32), -6.0, 6.0)
    return drawn.astype(jnp.bfloat16)


def level_of(stream_key, shape, cuts, low, largest):
    def one(dim, parts):
        draws = jax.random.uniform(jax.random.fold_in(jax.random.fold_in(stream_key, 6), dim), (parts,), jnp.float32, low / len(cuts), largest / len(cuts))
        return jnp.repeat(jnp.exp(draws), shape[dim] // parts).reshape((-1,) + (1,) * (len(shape) - dim - 1))

    level = one(*cuts[0])
    for cut in cuts[1:]:
        level = level * one(*cut)
    return level


def bell_draw(key, extent, scale, most, shards=(), held_as=jnp.bfloat16):
    values = scale * jax.random.normal(key, extent, jnp.float32)
    if shards:
        values = values * level_of(key, extent, shards, -0.22, 0.18)
    return jnp.clip(values, -most, most).astype(held_as)


def setup_inputs(seed: int = 0) -> dict:
    key_of = jax.random.split(jax.random.key(seed), 15)
    tokens = bell_draw(key_of[0], (REQUESTS, BLOCK, D), 1.0, 6.0, ((0, 32),))
    cache_kv = draw_cache_kv(jax.random.fold_in(key_of[14], 71), 0)
    cache_len = draw_cache_len(jax.random.fold_in(key_of[14], 71), 0)
    holder = draw_holder(jax.random.fold_in(key_of[14], 71), 0)
    accept = draw_accept(jax.random.fold_in(key_of[14], 71), 0)
    attn_gain = jnp.clip(1.0 + 0.18 * jax.random.normal(key_of[5], (D,), jnp.float32), 0.1, 1.9)
    q_weight = bell_draw(key_of[6], (D, QW), D ** -0.5, 0.15625)
    k_weight = bell_draw(key_of[7], (D, KVW), D ** -0.5, 0.15625)
    v_weight = bell_draw(key_of[8], (D, KVW), D ** -0.5, 0.15625)
    o_weight = bell_draw(key_of[9], (QW, D), QW ** -0.5, 0.21875)
    ffn_gain = jnp.clip(jnp.exp(jax.random.uniform(key_of[10], (D,), jnp.float32, math.log(0.4), math.log(2.5))), 0.4, 2.5)
    w_gate = bell_draw(key_of[11], (D, FF), D ** -0.5, 0.15625, ((1, 16),))
    w_up = bell_draw(key_of[12], (D, FF), D ** -0.5, 0.15625, ((1, 16),))
    w_down = bell_draw(key_of[13], (FF, D), FF ** -0.5, 0.09375, ((0, 16),))
    return dict(tokens=tokens, cache_kv=cache_kv, cache_len=cache_len, holder=holder, accept=accept, attn_gain=attn_gain, q_weight=q_weight, k_weight=k_weight, v_weight=v_weight, o_weight=o_weight, ffn_gain=ffn_gain, w_gate=w_gate, w_up=w_up, w_down=w_down)


norm_eps = 1e-05
rope_base = 100000.0

def rms_scale(values, gain_row):
    return values * lax.rsqrt(lax.optimization_barrier(jnp.mean(values * values, axis=-1, keepdims=True)) + norm_eps) * gain_row

def rotate_heads(flat, positions, head_count):
    half_dim = HEAD // 2
    shaped = flat.reshape(flat.shape[0], head_count, HEAD)
    freqs = jnp.exp(-jnp.log(rope_base) * 2.0 * jnp.arange(half_dim, dtype=jnp.float32) / HEAD)
    angles = positions[:, None] * freqs[None, :]
    cosine = jnp.cos(angles)[:, None, :]
    sine = jnp.sin(angles)[:, None, :]
    first_half = shaped[..., :half_dim]
    second_half = shaped[..., half_dim:]
    turned = jnp.concatenate([first_half * cosine - second_half * sine, second_half * cosine + first_half * sine], axis=-1)
    return turned.reshape(flat.shape[0], head_count * HEAD)

def attend_block(tok_rows, cache_keys, cache_vals, cache_length, attn_gain, q_weight, k_weight, v_weight, o_weight):
    block_len = tok_rows.shape[0]
    slot_len = cache_keys.shape[0]
    widened = tok_rows.astype(jnp.float32)
    normed = rms_scale(widened, attn_gain).astype(jnp.bfloat16)
    positions = (cache_length + jnp.arange(block_len, dtype=jnp.int32)).astype(jnp.float32)
    queries = rotate_heads(jnp.dot(normed, q_weight, preferred_element_type=jnp.float32), positions, HEADS).astype(jnp.bfloat16)
    new_keys = rotate_heads(jnp.dot(normed, k_weight, preferred_element_type=jnp.float32), positions, KV_HEADS).astype(jnp.bfloat16)
    new_vals = jnp.dot(normed, v_weight, preferred_element_type=jnp.float32).astype(jnp.bfloat16)
    all_keys = jnp.concatenate([cache_keys, new_keys], axis=0).reshape(slot_len + block_len, KV_HEADS, HEAD)
    all_vals = jnp.concatenate([cache_vals, new_vals], axis=0).reshape(slot_len + block_len, KV_HEADS, HEAD)
    grouped = queries.reshape(block_len, KV_HEADS, HEADS // KV_HEADS, HEAD)
    scores = jnp.einsum('bgid,kgd->gibk', grouped.astype(jnp.float32), all_keys.astype(jnp.float32)) * HEAD ** (-0.5)
    valid = jnp.concatenate([jnp.arange(slot_len, dtype=jnp.int32) < cache_length, jnp.ones((block_len,), dtype=jnp.bool_)])
    scores = jnp.where(valid, scores, -jnp.inf)
    peaks = lax.optimization_barrier(jnp.max(scores, axis=-1, keepdims=True))
    expd = jnp.exp(scores - peaks)
    probs = (expd / lax.optimization_barrier(jnp.sum(expd, axis=-1, keepdims=True))).astype(jnp.bfloat16)
    context = jnp.einsum('gibk,kgd->bgid', probs.astype(jnp.float32), all_vals.astype(jnp.float32))
    context = context.astype(jnp.bfloat16).reshape(block_len, HEADS * HEAD)
    return widened + jnp.dot(context, o_weight, preferred_element_type=jnp.float32)

def reference(tokens, cache_kv, cache_len, holder, accept, attn_gain, q_weight, k_weight, v_weight, o_weight, ffn_gain, w_gate, w_up, w_down):
    source = holder * BLK_GROUP + jnp.arange(REQUESTS, dtype=jnp.int32) % BLK_GROUP
    fetched = cache_kv[source]
    cache_keys = fetched[:, 0]
    cache_vals = fetched[:, 1]

    def one_pass(states):
        return jax.vmap(attend_block, in_axes=(0, 0, 0, 0, None, None, None, None, None))(states, cache_keys, cache_vals, cache_len, attn_gain, q_weight, k_weight, v_weight, o_weight)
    first = one_pass(tokens)
    flat_first = first.reshape(REQUESTS * BLOCK, D)
    fnorm = rms_scale(flat_first, ffn_gain).astype(jnp.bfloat16)

    def add_group(total, group_index):
        offset = group_index * FF_DEV
        gate_cols = lax.dynamic_slice_in_dim(w_gate, offset, FF_DEV, 1)
        up_cols = lax.dynamic_slice_in_dim(w_up, offset, FF_DEV, 1)
        down_rows = lax.dynamic_slice_in_dim(w_down, offset, FF_DEV, 0)
        gate_vals = jnp.dot(fnorm, gate_cols, preferred_element_type=jnp.float32)
        up_vals = jnp.dot(fnorm, up_cols, preferred_element_type=jnp.float32)
        hidden = (jax.nn.silu(gate_vals) * up_vals).astype(jnp.bfloat16)
        partial_term = jnp.dot(hidden, down_rows, preferred_element_type=jnp.float32).astype(jnp.bfloat16)
        partial_term = lax.optimization_barrier(partial_term)
        return (total + partial_term.astype(jnp.float32), None)
    ffn_out, _ = lax.scan(add_group, jnp.zeros((REQUESTS * BLOCK, D), jnp.float32), jnp.arange(BLK_GROUP, dtype=jnp.int32))
    draft = (flat_first + ffn_out).reshape(REQUESTS, BLOCK, D)
    second_in = jnp.where((accept == 1)[:, :, None], draft, tokens.astype(jnp.float32))
    return one_pass(second_in)
```

```python
import functools

import jax
import jax.numpy as jnp
from jax import lax
from jax.experimental import pallas as pl
from jax.experimental.pallas import tpu as pltpu
from jax.sharding import PartitionSpec as P

HEAD = 96
ACCEPT = 64

norm_eps = 1e-05
rope_base = 100000.0


def rms_scale(values, gain_row):
    return (
        values * lax.rsqrt(jnp.mean(values * values, axis=-1, keepdims=True) + norm_eps) * gain_row
    )


def rotate_heads(flat, cosine, sine):
    half_dim = HEAD // 2
    shaped = flat.reshape(flat.shape[0], -1, HEAD)
    cosine, sine = cosine[:, None, :], sine[:, None, :]
    first_half = shaped[..., :half_dim]
    second_half = shaped[..., half_dim:]
    turned = jnp.concatenate(
        [first_half * cosine - second_half * sine, second_half * cosine + first_half * sine],
        axis=-1,
    )
    return turned.reshape(flat.shape)


def attend(queries, all_keys, all_vals, valid, o_weight):
    kv_count = all_keys.shape[1] // HEAD
    rows = queries.shape[0]
    grouped = queries.reshape(rows, kv_count, -1, HEAD)
    keys = all_keys.reshape(-1, kv_count, HEAD)
    vals = all_vals.reshape(-1, kv_count, HEAD)
    scores = jnp.einsum(
        "bgid,kgd->gibk", grouped, keys, preferred_element_type=jnp.float32
    ) * HEAD ** (-0.5)
    scores = jnp.where(valid, scores, -jnp.inf)
    peaks = jnp.max(scores, axis=-1, keepdims=True)
    expd = jnp.exp(scores - peaks)
    probs = (expd / jnp.sum(expd, axis=-1, keepdims=True)).astype(jnp.bfloat16)
    context = jnp.einsum("gibk,kgd->bgid", probs, vals, preferred_element_type=jnp.float32)
    context = context.astype(jnp.bfloat16).reshape(rows, -1)
    return jnp.dot(context, o_weight, preferred_element_type=jnp.float32)


def ffn_kernel(
    A, B, x_ref, wg_ref, wu_ref, wd_ref, out_ref,
    ag, own, core_st, core_land, y_st, y_land, z_st, z_land,
    ag_send, ag_recv, core_send, core_recv, y_send, y_recv, z_send, z_recv,
):
    R = x_ref.shape[0]
    me = lax.axis_index("blk")
    c = lax.rem(me, 2)
    b = lax.rem(me // 2, B)
    a = me // (2 * B)

    def dev(ra, rb, rc):
        na = lax.rem(a + ra, A)
        nb = lax.rem(b + rb, B)
        nc = lax.rem(c + rc, 2)
        return {"blk": (na * B + nb) * 2 + nc}

    peers = [dev(ra, 0, 0) for ra in range(1, A)]
    peers += [dev(0, rb, 0) for rb in range(1, B)]
    peers += [dev(0, 0, 1)]
    barrier = pltpu.get_barrier_semaphore()
    for peer in peers:
        pl.semaphore_signal(barrier, inc=1, device_id=peer, device_id_type=pl.DeviceIdType.MESH)

    started = []

    def send(src, dst, ssem, rsem, to):
        copy = pltpu.make_async_remote_copy(
            src_ref=src, dst_ref=dst, send_sem=ssem, recv_sem=rsem,
            device_id=to, device_id_type=pl.DeviceIdType.MESH,
        )
        copy.start()
        started.append(copy)

    def arrived(dst, rsem):
        pltpu.make_async_copy(dst, dst, rsem).wait()

    def sid(ra, rb, rc):
        return (ra * B + rb) * 2 + rc

    def cid(ra, rb):
        return ra * B + rb

    def ag_slot(ra, rb, rc):
        return ag.at[cid(ra, rb), pl.ds(rc * R, R)]

    n_ag = [0]

    def ag_copy(src, slot, to):
        i = n_ag[0]
        n_ag[0] += 1
        send(ag_slot(*src), ag_slot(*slot), ag_send.at[i], ag_recv.at[sid(*slot)], to)

    def to_core(ra, rb):
        ag_copy((ra, rb, 0), (ra, rb, 1), dev(0, 0, 1))

    def to_y(ra):
        for db in range(1, B):
            ag_copy((ra, 0, 0), (ra, B - db, 0), dev(0, db, 0))

    ag[0, pl.ds(0, R)] = x_ref[...]
    pl.semaphore_wait(barrier, len(peers))

    zorder = sorted(range(1, A), key=lambda r: min(r, A - r))
    to_core(0, 0)
    to_y(0)
    for da in zorder:
        ag_copy((0, 0, 0), (A - da, 0, 0), dev(da, 0, 0))

    order = [(0, 0)] + [(0, rb) for rb in range(1, B)] + [(ra, 0) for ra in zorder]
    order += [(ra, rb) for ra in zorder for rb in range(1, B)]

    def arrive(ra, rb):
        if (ra, rb) == (0, 0):
            return
        arrived(ag_slot(ra, rb, 0), ag_recv.at[sid(ra, rb, 0)])
        if rb == 0:
            to_y(ra)
        to_core(ra, rb)

    def compute(ra, rb):
        i = cid(ra, rb)
        arrived(ag_slot(ra, rb, 1), ag_recv.at[sid(ra, rb, 1)])
        x = ag[i]
        gate = jnp.dot(x, wg_ref[...], preferred_element_type=jnp.float32)
        up = jnp.dot(x, wu_ref[...], preferred_element_type=jnp.float32)
        hidden = (gate / (1.0 + jnp.exp(-gate)) * up).astype(jnp.bfloat16)
        term = jnp.dot(hidden, wd_ref[...], preferred_element_type=jnp.float32)
        term = term.astype(jnp.bfloat16)
        own[i] = term[:R]
        core_st[i] = term[R:]
        send(core_st.at[i], core_land.at[i], core_send.at[i], core_recv.at[i], dev(0, 0, 1))

    def chip_sum(ra, rb):
        i = cid(ra, rb)
        arrived(core_land.at[i], core_recv.at[i])
        return own[i].astype(jnp.float32) + core_land[i].astype(jnp.float32)

    def y_step(ra, rb):
        i = cid(ra, rb)
        j = cid(ra, B - rb)
        y_st[i] = chip_sum(ra, rb).astype(jnp.bfloat16)
        send(y_st.at[i], y_land.at[j], y_send.at[i], y_recv.at[j], dev(0, rb, 0))

    def line_sum(ra):
        total = chip_sum(ra, 0)
        for rb in range(1, B):
            j = cid(ra, rb)
            arrived(y_land.at[j], y_recv.at[j])
            total = total + y_land[j].astype(jnp.float32)
        return total

    def z_step(ra):
        z_st[ra] = line_sum(ra).astype(jnp.bfloat16)
        send(z_st.at[ra], z_land.at[A - ra], z_send.at[ra], z_recv.at[A - ra], dev(ra, 0, 0))

    for k, pair in enumerate(order):
        if 0 < k and k + 1 < len(order):
            arrive(*order[k + 1])
        elif k == 0:
            pass
        compute(*pair)
        if k == 0:
            arrive(*order[1])
        if k >= 1 and order[k - 1][1]:
            y_step(*order[k - 1])
    if order[-1][1]:
        y_step(*order[-1])
    for ra in zorder:
        z_step(ra)
    total = line_sum(0)
    for ra in range(1, A):
        arrived(z_land.at[ra], z_recv.at[ra])
        total = total + z_land[ra].astype(jnp.float32)
    out_ref[...] = total
    for copy in started:
        copy.wait_send()


def run_ffn(x, w_gate, w_up, w_down, count):
    R, D = x.shape
    A = 4
    B = count // (2 * A)
    pairs = A * B
    block = lambda n: pltpu.VMEM((n, R, D), jnp.bfloat16)
    dma = pltpu.SemaphoreType.DMA
    return pl.pallas_call(
        functools.partial(ffn_kernel, A, B),
        out_shape=jax.ShapeDtypeStruct((R, D), jnp.float32),
        in_specs=[pl.BlockSpec(memory_space=pltpu.VMEM)] * 4,
        out_specs=pl.BlockSpec(memory_space=pltpu.VMEM),
        scratch_shapes=[
            pltpu.VMEM((pairs, 2 * R, D), jnp.bfloat16),
            block(pairs), block(pairs), block(pairs), block(pairs), block(pairs),
            block(A), block(A),
            dma((2 * pairs,)), dma((2 * pairs,)),
            dma((pairs,)), dma((pairs,)), dma((pairs,)), dma((pairs,)),
            dma((A,)), dma((A,)),
        ],
        compiler_params=pltpu.CompilerParams(
            collective_id=0, has_side_effects=True, vmem_limit_bytes=56 * 2**20
        ),
    )(x, w_gate, w_up, w_down)


def local(
    count,
    tokens,
    cache_kv,
    cache_len,
    holder,
    accept,
    attn_gain,
    q_weight,
    k_weight,
    v_weight,
    o_weight,
    ffn_gain,
    w_gate,
    w_up,
    w_down,
):
    f32, bf16 = jnp.float32, jnp.bfloat16
    own_holder = holder[0]
    slots = lax.all_gather(cache_kv, "req", axis=0, tiled=True)
    matches = jnp.arange(slots.shape[0], dtype=jnp.int32) == own_holder
    fetched = jnp.sum(
        jnp.where(matches[:, None, None, None], slots, jnp.zeros_like(slots)), axis=0
    )
    cache_keys, cache_vals = fetched[0], fetched[1]
    cache_length = cache_len[0]
    block_rows = tokens[0]
    n = block_rows.shape[0]

    chosen = accept[0] == 1
    at = jnp.arange(n, dtype=jnp.int32)
    before = at[None, :] <= at[:, None]
    count_in = jnp.sum(jnp.where(before & chosen[None, :], 1, 0), axis=1)
    place = jnp.where(chosen, count_in - 1, ACCEPT + at - count_in)
    move = place[None, :] == at[:, None]
    x = jnp.dot(move.astype(bf16), block_rows, preferred_element_type=f32)
    positions = cache_length + jnp.sum(jnp.where(move, at[None, :], 0), axis=1)
    freqs = jnp.exp(
        -jnp.log(rope_base) * 2.0 * jnp.arange(HEAD // 2, dtype=f32) / HEAD
    )
    angles = positions.astype(f32)[:, None] * freqs[None, :]
    cosine, sine = jnp.cos(angles), jnp.sin(angles)
    valid = jnp.concatenate(
        [
            jnp.arange(cache_keys.shape[0], dtype=jnp.int32) < cache_length,
            jnp.ones((n,), dtype=jnp.bool_),
        ]
    )

    def project(rows, weight):
        return jnp.dot(rows, weight, preferred_element_type=f32)

    normed = rms_scale(x, attn_gain).astype(bf16)
    q1 = rotate_heads(project(normed, q_weight), cosine, sine).astype(bf16)
    k1 = rotate_heads(project(normed, k_weight), cosine, sine).astype(bf16)
    v1 = project(normed, v_weight).astype(bf16)
    first = x[:ACCEPT] + attend(
        q1[:ACCEPT],
        jnp.concatenate([cache_keys, k1]),
        jnp.concatenate([cache_vals, v1]),
        valid,
        o_weight,
    )
    ffn = run_ffn(rms_scale(first, ffn_gain).astype(bf16), w_gate, w_up, w_down, count)
    draft = first + ffn
    normed2 = rms_scale(draft, attn_gain).astype(bf16)
    c2, s2 = cosine[:ACCEPT], sine[:ACCEPT]
    q2 = rotate_heads(project(normed2, q_weight), c2, s2).astype(bf16)
    k2 = rotate_heads(project(normed2, k_weight), c2, s2).astype(bf16)
    v2 = project(normed2, v_weight).astype(bf16)
    second = jnp.concatenate([draft, x[ACCEPT:]])
    refined = second + attend(
        jnp.concatenate([q2, q1[ACCEPT:]]),
        jnp.concatenate([cache_keys, k2, k1[ACCEPT:]]),
        jnp.concatenate([cache_vals, v2, v1[ACCEPT:]]),
        valid,
        o_weight,
    )
    back = (place[:, None] == at[None, :]).astype(f32)
    return jnp.dot(back, refined, precision=lax.Precision.HIGHEST)[None]


def solution(mesh):
    return jax.shard_map(
        functools.partial(local, mesh.shape["blk"]),
        mesh=mesh,
        in_specs=(
            P(("req", "blk"), None, None),
            P(("req", "blk"), None, None, None),
            P(("req", "blk")),
            P(("req", "blk")),
            P(("req", "blk"), None),
            P(),
            P(),
            P(),
            P(),
            P(),
            P(),
            P(None, "blk"),
            P(None, "blk"),
            P("blk", None),
        ),
        out_specs=P(("req", "blk"), None, None),
        check_vma=False,
    )
```

```python
import functools

import jax
import jax.numpy as jnp
from jax import lax
from jax.experimental import pallas as pl
from jax.experimental.pallas import tpu as pltpu
from jax.sharding import PartitionSpec as P

HEAD = 96
ACCEPT = 64

norm_eps = 1e-05
rope_base = 100000.0


def rms_scale(values, gain_row):
    return (
        values * lax.rsqrt(jnp.mean(values * values, axis=-1, keepdims=True) + norm_eps) * gain_row
    )


def dot(x, y):
    return jnp.dot(x, y, preferred_element_type=jnp.float32)


def pick(mask, values):
    high = values.astype(jnp.bfloat16)
    rest = values - high.astype(jnp.float32)
    mid = rest.astype(jnp.bfloat16)
    low = (rest - mid.astype(jnp.float32)).astype(jnp.bfloat16)
    return dot(mask, high) + dot(mask, mid) + dot(mask, low)


def rotate(flat, cosine, sine):
    width = flat.shape[1]
    half = HEAD // 2
    lane = lax.broadcasted_iota(jnp.int32, flat.shape, 1)
    ahead = pltpu.roll(flat, width - half, 1)
    behind = pltpu.roll(flat, half, 1)
    other = jnp.where(lane % HEAD < half, ahead, behind)
    return (flat * cosine + other * sine).astype(jnp.bfloat16)


def attend(q, kc, vc, kn, vn, length):
    rows = q.shape[0]
    kv_count = kc.shape[1] // HEAD
    group = q.shape[1] // HEAD // kv_count
    nt = (((1,), (1,)), ((), ()))
    outs = []
    for g in range(kv_count):
        cols = slice(g * HEAD, (g + 1) * HEAD)
        qs = jnp.concatenate(
            [q[:, (g * group + i) * HEAD : (g * group + i + 1) * HEAD] for i in range(group)]
        )
        sc = lax.dot_general(qs, kc[:, cols], nt, preferred_element_type=jnp.float32)
        sn = lax.dot_general(qs, kn[:, cols], nt, preferred_element_type=jnp.float32)
        lane = lax.broadcasted_iota(jnp.int32, sc.shape, 1)
        sc = jnp.where(lane < length, sc * HEAD ** (-0.5), -jnp.inf)
        sn = sn * HEAD ** (-0.5)
        peak = jnp.maximum(
            jnp.max(sc, axis=-1, keepdims=True), jnp.max(sn, axis=-1, keepdims=True)
        )
        ec, en = jnp.exp(sc - peak), jnp.exp(sn - peak)
        total = jnp.sum(ec, axis=-1, keepdims=True) + jnp.sum(en, axis=-1, keepdims=True)
        scale = 1.0 / total
        pc, pn = (ec * scale).astype(jnp.bfloat16), (en * scale).astype(jnp.bfloat16)
        ctx = dot(pc, vc[:, cols]) + dot(pn, vn[:, cols])
        outs += [ctx[i * rows : (i + 1) * rows] for i in range(group)]
    return jnp.concatenate(outs, axis=1).astype(jnp.bfloat16)


def layer_kernel(
    A, B, G, length_ref, holder_ref, accept_ref, tokens_ref, cos_ref, sin_ref, again_ref, fgain_ref,
    cache_hbm, wq_hbm, wk_hbm, wv_hbm, wo_hbm, wg_hbm, wu_hbm, wd_hbm, out_ref,
    wq_ref, wk_ref, wv_ref, wo_ref, wg_ref, wu_ref, wd_ref, slots, kc_ref, vc_ref,
    q_ref, kn_ref, vn_ref, x_ref, cosp, sinp, load_sem, slot_send, slot_recv,
    ag, own, core_st, core_land, y_st, y_land, z_st, z_land,
    ag_send, ag_recv, core_send, core_recv, y_send, y_recv, z_send, z_recv,
):
    R = ACCEPT
    f32, bf16 = jnp.float32, jnp.bfloat16
    n = tokens_ref.shape[0]
    loads = [
        pltpu.make_async_copy(s, d, load_sem.at[i])
        for i, (s, d) in enumerate(
            [(wq_hbm, wq_ref), (wk_hbm, wk_ref), (wv_hbm, wv_ref), (cache_hbm, slots.at[0]),
             (wo_hbm, wo_ref), (wg_hbm, wg_ref), (wu_hbm, wu_ref), (wd_hbm, wd_ref)]
        )
    ]
    for load in loads:
        load.start()
    req = lax.axis_index("req")
    me = lax.axis_index("blk")
    c = lax.rem(me, 2)
    b = lax.rem(me // 2, B)
    a = me // (2 * B)

    def dev(ra, rb, rc):
        na = lax.rem(a + ra, A)
        nb = lax.rem(b + rb, B)
        nc = lax.rem(c + rc, 2)
        return {"blk": (na * B + nb) * 2 + nc}

    def column(r):
        return {"req": lax.rem(req + r, G)}

    peers = [dev(ra, 0, 0) for ra in range(1, A)]
    peers += [dev(0, rb, 0) for rb in range(1, B)]
    peers += [dev(0, 0, 1)]
    peers += [column(r) for r in range(1, G)]
    barrier = pltpu.get_barrier_semaphore()
    for peer in peers:
        pl.semaphore_signal(barrier, inc=1, device_id=peer, device_id_type=pl.DeviceIdType.MESH)

    started = []

    def send(src, dst, ssem, rsem, to):
        copy = pltpu.make_async_remote_copy(
            src_ref=src, dst_ref=dst, send_sem=ssem, recv_sem=rsem,
            device_id=to, device_id_type=pl.DeviceIdType.MESH,
        )
        copy.start()
        started.append(copy)

    def arrived(dst, rsem):
        pltpu.make_async_copy(dst, dst, rsem).wait()

    def sid(ra, rb, rc):
        return (ra * B + rb) * 2 + rc

    def cid(ra, rb):
        return ra * B + rb

    def ag_slot(ra, rb, rc):
        return ag.at[cid(ra, rb), pl.ds(rc * R, R)]

    n_ag = [0]

    def ag_copy(src, slot, to):
        i = n_ag[0]
        n_ag[0] += 1
        send(ag_slot(*src), ag_slot(*slot), ag_send.at[i], ag_recv.at[sid(*slot)], to)

    def to_core(ra, rb):
        ag_copy((ra, rb, 0), (ra, rb, 1), dev(0, 0, 1))

    def to_y(ra):
        for db in range(1, B):
            ag_copy((ra, 0, 0), (ra, B - db, 0), dev(0, db, 0))

    pl.semaphore_wait(barrier, len(peers))
    for r in range(1, G):
        send(cache_hbm, slots.at[G - r], slot_send.at[r], slot_recv.at[G - r], column(r))

    chosen = accept_ref[...] == 1
    row = lax.broadcasted_iota(jnp.int32, (n, n), 0)
    col = lax.broadcasted_iota(jnp.int32, (n, n), 1)
    tri = jnp.where(row <= col, 1.0, 0.0).astype(bf16)
    taken = jnp.broadcast_to(jnp.where(chosen, 1.0, 0.0), (16, n)).astype(bf16)
    upto = dot(taken, tri)[:1].astype(jnp.int32)
    at = lax.broadcasted_iota(jnp.int32, (1, n), 1)
    place = jnp.where(chosen, upto - 1, R + at - upto)
    move32 = jnp.where(row == place, 1.0, 0.0)
    move = move32.astype(bf16)
    x_ref[...] = dot(move, tokens_ref[...])
    cosp[...] = pick(move, cos_ref[...])
    sinp[...] = pick(move, sin_ref[...])
    length = length_ref[0]
    kw = kn_ref.shape[1]

    normed = rms_scale(x_ref[...], again_ref[...]).astype(bf16)
    loads[0].wait()
    q_ref[...] = rotate(dot(normed, wq_ref[...]), cosp[...], sinp[...])
    loads[1].wait()
    kn_ref[...] = rotate(dot(normed, wk_ref[...]), cosp[:, :kw], sinp[:, :kw])
    loads[2].wait()
    vn_ref[...] = dot(normed, wv_ref[...]).astype(bf16)

    loads[3].wait()
    kc, vc = slots[0, 0], slots[0, 1]
    for r in range(1, G):
        arrived(slots.at[r], slot_recv.at[r])
        here = lax.rem(req + r, G) == holder_ref[0]
        kc = jnp.where(here, slots[r, 0], kc)
        vc = jnp.where(here, slots[r, 1], vc)
    kc_ref[...] = kc
    vc_ref[...] = vc

    ctx = attend(q_ref[:R], kc_ref[...], vc_ref[...], kn_ref[...], vn_ref[...], length)
    loads[4].wait()
    first = x_ref[:R] + dot(ctx, wo_ref[...])
    x_ref[:R] = first
    ag[0, pl.ds(0, R)] = rms_scale(first, fgain_ref[...]).astype(bf16)

    up_steps = A // 2
    down_steps = A - 1 - up_steps
    zorder = []
    for k in range(1, up_steps + 1):
        zorder.append(A - k)
        if k <= down_steps:
            zorder.append(k)

    def to_z(ra):
        k = (A - ra) % A
        if k < up_steps and (ra == 0 or ra > down_steps):
            ag_copy((ra, 0, 0), ((ra - 1) % A, 0, 0), dev(1, 0, 0))
        if ra < down_steps:
            ag_copy((ra, 0, 0), (ra + 1, 0, 0), dev(A - 1, 0, 0))

    to_z(0)
    to_y(0)
    to_core(0, 0)
    for load in loads[5:]:
        load.wait()

    order = [(0, 0)] + [(0, rb) for rb in range(1, B)] + [(ra, 0) for ra in zorder]
    order += [(ra, rb) for ra in zorder for rb in range(1, B)]

    def arrive(ra, rb):
        if (ra, rb) == (0, 0):
            return
        arrived(ag_slot(ra, rb, 0), ag_recv.at[sid(ra, rb, 0)])
        if rb == 0:
            to_z(ra)
            to_y(ra)
        to_core(ra, rb)

    def compute(ra, rb):
        i = cid(ra, rb)
        arrived(ag_slot(ra, rb, 1), ag_recv.at[sid(ra, rb, 1)])
        x = ag[i]
        gate = jnp.dot(x, wg_ref[...], preferred_element_type=jnp.float32)
        up = jnp.dot(x, wu_ref[...], preferred_element_type=jnp.float32)
        hidden = (gate / (1.0 + jnp.exp(-gate)) * up).astype(jnp.bfloat16)
        term = jnp.dot(hidden, wd_ref[...], preferred_element_type=jnp.float32)
        term = term.astype(jnp.bfloat16)
        own[i] = term[:R]
        core_st[i] = term[R:]
        send(core_st.at[i], core_land.at[i], core_send.at[i], core_recv.at[i], dev(0, 0, 1))

    def chip_sum(ra, rb):
        i = cid(ra, rb)
        arrived(core_land.at[i], core_recv.at[i])
        return own[i].astype(jnp.float32) + core_land[i].astype(jnp.float32)

    def y_step(ra, rb):
        i = cid(ra, rb)
        j = cid(ra, B - rb)
        y_st[i] = chip_sum(ra, rb).astype(jnp.bfloat16)
        send(y_st.at[i], y_land.at[j], y_send.at[i], y_recv.at[j], dev(0, rb, 0))

    def line_sum(ra):
        total = chip_sum(ra, 0)
        for rb in range(1, B):
            j = cid(ra, rb)
            arrived(y_land.at[j], y_recv.at[j])
            total = total + y_land[j].astype(jnp.float32)
        return total

    def z_step(ra):
        z_st[ra] = line_sum(ra).astype(jnp.bfloat16)
        send(z_st.at[ra], z_land.at[A - ra], z_send.at[ra], z_recv.at[A - ra], dev(ra, 0, 0))

    for k, pair in enumerate(order):
        if 0 < k and k + 1 < len(order):
            arrive(*order[k + 1])
        elif k == 0:
            pass
        compute(*pair)
        if k == 0:
            arrive(*order[1])
        if k >= 1 and order[k - 1][1]:
            y_step(*order[k - 1])
    if order[-1][1]:
        y_step(*order[-1])
    for ra in zorder:
        z_step(ra)
    total = line_sum(0)
    for ra in range(1, A):
        arrived(z_land.at[ra], z_recv.at[ra])
        total = total + z_land[ra].astype(jnp.float32)
    draft = x_ref[:R] + total
    x_ref[:R] = draft
    normed = rms_scale(draft, again_ref[...]).astype(bf16)
    q_ref[:R] = rotate(dot(normed, wq_ref[...]), cosp[:R], sinp[:R])
    kn_ref[:R] = rotate(dot(normed, wk_ref[...]), cosp[:R, :kw], sinp[:R, :kw])
    vn_ref[:R] = dot(normed, wv_ref[...]).astype(bf16)
    ctx = attend(q_ref[...], kc_ref[...], vc_ref[...], kn_ref[...], vn_ref[...], length)
    refined = x_ref[...] + dot(ctx, wo_ref[...])
    out_ref[...] = pick(move32.T.astype(bf16), refined)
    for copy in started:
        copy.wait_send()


def local(
    mesh_shape,
    tokens,
    cache_kv,
    cache_len,
    holder,
    accept,
    attn_gain,
    q_weight,
    k_weight,
    v_weight,
    o_weight,
    ffn_gain,
    w_gate,
    w_up,
    w_down,
):
    f32, bf16 = jnp.float32, jnp.bfloat16
    n, D = tokens.shape[1:]
    qw, kw = q_weight.shape[1], k_weight.shape[1]
    cs = cache_kv.shape[2]
    positions = (cache_len[0] + jnp.arange(n, dtype=jnp.int32)).astype(f32)
    lane = jnp.arange(qw, dtype=jnp.int32) % HEAD
    half = HEAD // 2
    freqs = jnp.exp(-jnp.log(rope_base) * 2.0 * (lane % half).astype(f32) / HEAD)
    angles = positions[:, None] * freqs[None, :]
    cosine = jnp.cos(angles)
    sine = jnp.where(lane < half, -1.0, 1.0) * jnp.sin(angles)
    R = ACCEPT
    A = 4
    B = mesh_shape["blk"] // (2 * A)
    G = mesh_shape["req"]
    pairs = A * B
    block = lambda m: pltpu.VMEM((m, R, D), bf16)
    dma = pltpu.SemaphoreType.DMA
    vmem = pl.BlockSpec(memory_space=pltpu.VMEM)
    smem = pl.BlockSpec(memory_space=pltpu.SMEM)
    anys = pl.BlockSpec(memory_space=pl.ANY)
    held = lambda w: pltpu.VMEM(w.shape, w.dtype)
    out = pl.pallas_call(
        functools.partial(layer_kernel, A, B, G),
        out_shape=jax.ShapeDtypeStruct((n, D), f32),
        in_specs=[smem] * 2 + [vmem] * 6 + [anys] * 8,
        out_specs=vmem,
        scratch_shapes=[
            held(q_weight), held(k_weight), held(v_weight), held(o_weight),
            held(w_gate), held(w_up), held(w_down),
            pltpu.VMEM((G, 2, cs, kw), bf16),
            pltpu.VMEM((cs, kw), bf16), pltpu.VMEM((cs, kw), bf16),
            pltpu.VMEM((n, qw), bf16), pltpu.VMEM((n, kw), bf16), pltpu.VMEM((n, kw), bf16),
            pltpu.VMEM((n, D), f32), pltpu.VMEM((n, qw), f32), pltpu.VMEM((n, qw), f32),
            dma((8,)), dma((G,)), dma((G,)),
            pltpu.VMEM((pairs, 2 * R, D), bf16),
            block(pairs), block(pairs), block(pairs), block(pairs), block(pairs),
            block(A), block(A),
            dma((2 * pairs,)), dma((2 * pairs,)),
            dma((pairs,)), dma((pairs,)), dma((pairs,)), dma((pairs,)),
            dma((A,)), dma((A,)),
        ],
        compiler_params=pltpu.CompilerParams(
            collective_id=0, has_side_effects=True, vmem_limit_bytes=58 * 2**20
        ),
    )(
        cache_len, holder, accept, tokens[0], cosine, sine, attn_gain[None], ffn_gain[None],
        cache_kv[0], q_weight, k_weight, v_weight, o_weight, w_gate, w_up, w_down,
    )
    return out[None]


def solution(mesh):
    return jax.shard_map(
        functools.partial(local, dict(mesh.shape)),
        mesh=mesh,
        in_specs=(
            P(("req", "blk"), None, None),
            P(("req", "blk"), None, None, None),
            P(("req", "blk")),
            P(("req", "blk")),
            P(("req", "blk"), None),
            P(),
            P(),
            P(),
            P(),
            P(),
            P(),
            P(None, "blk"),
            P(None, "blk"),
            P("blk", None),
        ),
        out_specs=P(("req", "blk"), None, None),
        check_vma=False,
    )
```

```python
import functools

import jax
import jax.numpy as jnp
from jax import lax
from jax.experimental import pallas as pl
from jax.experimental.pallas import tpu as pltpu
from jax.sharding import PartitionSpec as P

HEAD = 96
ACCEPT = 64

norm_eps = 1e-05
rope_base = 100000.0


def rms_scale(values, gain_row):
    return (
        values * lax.rsqrt(jnp.mean(values * values, axis=-1, keepdims=True) + norm_eps) * gain_row
    )


def dot(x, y):
    return jnp.dot(x, y, preferred_element_type=jnp.float32)


def pick(mask, values):
    high = values.astype(jnp.bfloat16)
    rest = values - high.astype(jnp.float32)
    mid = rest.astype(jnp.bfloat16)
    low = (rest - mid.astype(jnp.float32)).astype(jnp.bfloat16)
    return dot(mask, high) + dot(mask, mid) + dot(mask, low)


def rotate(flat, cosine, sine):
    width = flat.shape[1]
    half = HEAD // 2
    lane = lax.broadcasted_iota(jnp.int32, flat.shape, 1)
    ahead = pltpu.roll(flat, width - half, 1)
    behind = pltpu.roll(flat, half, 1)
    other = jnp.where(lane % HEAD < half, ahead, behind)
    return (flat * cosine + other * sine).astype(jnp.bfloat16)


def attend(q, kc, vc, kn, vn, length):
    rows = q.shape[0]
    kv_count = kc.shape[1] // HEAD
    group = q.shape[1] // HEAD // kv_count
    nt = (((1,), (1,)), ((), ()))
    outs = []
    for g in range(kv_count):
        cols = slice(g * HEAD, (g + 1) * HEAD)
        qs = jnp.concatenate(
            [q[:, (g * group + i) * HEAD : (g * group + i + 1) * HEAD] for i in range(group)]
        )
        sc = lax.dot_general(qs, kc[:, cols], nt, preferred_element_type=jnp.float32)
        sn = lax.dot_general(qs, kn[:, cols], nt, preferred_element_type=jnp.float32)
        lane = lax.broadcasted_iota(jnp.int32, sc.shape, 1)
        sc = jnp.where(lane < length, sc * HEAD ** (-0.5), -jnp.inf)
        sn = sn * HEAD ** (-0.5)
        peak = jnp.maximum(
            jnp.max(sc, axis=-1, keepdims=True), jnp.max(sn, axis=-1, keepdims=True)
        )
        ec, en = jnp.exp(sc - peak), jnp.exp(sn - peak)
        total = jnp.sum(ec, axis=-1, keepdims=True) + jnp.sum(en, axis=-1, keepdims=True)
        scale = 1.0 / total
        pc, pn = (ec * scale).astype(jnp.bfloat16), (en * scale).astype(jnp.bfloat16)
        ctx = dot(pc, vc[:, cols]) + dot(pn, vn[:, cols])
        outs += [ctx[i * rows : (i + 1) * rows] for i in range(group)]
    return jnp.concatenate(outs, axis=1).astype(jnp.bfloat16)


def layer_kernel(
    A, B, G, length_ref, holder_ref, accept_ref, tokens_ref, cos_ref, sin_ref, again_ref, fgain_ref,
    cache_hbm, wq_hbm, wk_hbm, wv_hbm, wo_hbm, wg_hbm, wu_hbm, wd_hbm, out_ref,
    wq_ref, wk_ref, wv_ref, wo_ref, wg_ref, wu_ref, wd_ref, slots, kc_ref, vc_ref,
    q_ref, kn_ref, vn_ref, x_ref, cosp, sinp, load_sem, slot_send, slot_recv,
    ag, own, core_st, core_land, y_st, y_land, z_st, z_land,
    ag_send, ag_recv, core_send, core_recv, y_send, y_recv, z_send, z_recv,
):
    R = ACCEPT
    f32, bf16 = jnp.float32, jnp.bfloat16
    n = tokens_ref.shape[0]
    loads = [
        pltpu.make_async_copy(s, d, load_sem.at[i])
        for i, (s, d) in enumerate(
            [(wq_hbm, wq_ref), (wk_hbm, wk_ref), (wv_hbm, wv_ref), (cache_hbm, slots.at[0]),
             (wo_hbm, wo_ref), (wg_hbm, wg_ref), (wu_hbm, wu_ref), (wd_hbm, wd_ref)]
        )
    ]
    for load in loads:
        load.start()
    req = lax.axis_index("req")
    me = lax.axis_index("blk")
    c = lax.rem(me, 2)
    b = lax.rem(me // 2, B)
    a = me // (2 * B)

    def dev(ra, rb, rc):
        na = lax.rem(a + ra, A)
        nb = lax.rem(b + rb, B)
        nc = lax.rem(c + rc, 2)
        return {"blk": (na * B + nb) * 2 + nc}

    def column(r):
        return {"req": lax.rem(req + r, G)}

    peers = [dev(ra, 0, 0) for ra in range(1, A)]
    peers += [dev(0, rb, 0) for rb in range(1, B)]
    peers += [dev(0, 0, 1)]
    peers += [column(r) for r in range(1, G)]
    barrier = pltpu.get_barrier_semaphore()
    for peer in peers:
        pl.semaphore_signal(barrier, inc=1, device_id=peer, device_id_type=pl.DeviceIdType.MESH)

    started = []

    def send(src, dst, ssem, rsem, to):
        copy = pltpu.make_async_remote_copy(
            src_ref=src, dst_ref=dst, send_sem=ssem, recv_sem=rsem,
            device_id=to, device_id_type=pl.DeviceIdType.MESH,
        )
        copy.start()
        started.append(copy)

    def arrived(dst, rsem):
        pltpu.make_async_copy(dst, dst, rsem).wait()

    def sid(ra, rb, rc):
        return (ra * B + rb) * 2 + rc

    def cid(ra, rb):
        return ra * B + rb

    def ag_slot(ra, rb, rc):
        return ag.at[cid(ra, rb), pl.ds(rc * R, R)]

    n_ag = [0]

    def ag_copy(src, slot, to):
        i = n_ag[0]
        n_ag[0] += 1
        send(ag_slot(*src), ag_slot(*slot), ag_send.at[i], ag_recv.at[sid(*slot)], to)

    def to_core(ra, rb):
        ag_copy((ra, rb, 0), (ra, rb, 1), dev(0, 0, 1))

    def to_y(ra):
        for db in range(1, B):
            ag_copy((ra, 0, 0), (ra, B - db, 0), dev(0, db, 0))

    pl.semaphore_wait(barrier, len(peers))
    for r in range(1, G):
        send(cache_hbm, slots.at[G - r], slot_send.at[r], slot_recv.at[G - r], column(r))

    chosen = accept_ref[...] == 1
    row = lax.broadcasted_iota(jnp.int32, (n, n), 0)
    col = lax.broadcasted_iota(jnp.int32, (n, n), 1)
    tri = jnp.where(row <= col, 1.0, 0.0).astype(bf16)
    taken = jnp.broadcast_to(jnp.where(chosen, 1.0, 0.0), (16, n)).astype(bf16)
    upto = dot(taken, tri)[:1].astype(jnp.int32)
    at = lax.broadcasted_iota(jnp.int32, (1, n), 1)
    place = jnp.where(chosen, upto - 1, R + at - upto)
    move32 = jnp.where(row == place, 1.0, 0.0)
    move = move32.astype(bf16)
    x_ref[...] = dot(move, tokens_ref[...])
    cosp[...] = pick(move, cos_ref[...])
    sinp[...] = pick(move, sin_ref[...])
    length = length_ref[0]
    kw = kn_ref.shape[1]

    normed = rms_scale(x_ref[...], again_ref[...][None]).astype(bf16)
    loads[0].wait()
    q_ref[...] = rotate(dot(normed, wq_ref[...]), cosp[...], sinp[...])
    loads[1].wait()
    kn_ref[...] = rotate(dot(normed, wk_ref[...]), cosp[:, :kw], sinp[:, :kw])
    loads[2].wait()
    vn_ref[...] = dot(normed, wv_ref[...]).astype(bf16)

    loads[3].wait()
    kc, vc = slots[0, 0], slots[0, 1]
    for r in range(1, G):
        arrived(slots.at[r], slot_recv.at[r])
        here = lax.rem(req + r, G) == holder_ref[0]
        kc = jnp.where(here, slots[r, 0], kc)
        vc = jnp.where(here, slots[r, 1], vc)
    kc_ref[...] = kc
    vc_ref[...] = vc

    ctx = attend(q_ref[:R], kc_ref[...], vc_ref[...], kn_ref[...], vn_ref[...], length)
    loads[4].wait()
    first = x_ref[:R] + dot(ctx, wo_ref[...])
    x_ref[:R] = first
    ag[0, pl.ds(0, R)] = rms_scale(first, fgain_ref[...][None]).astype(bf16)

    up_steps = A // 2
    down_steps = A - 1 - up_steps
    zorder = []
    for k in range(1, up_steps + 1):
        zorder.append(A - k)
        if k <= down_steps:
            zorder.append(k)

    def to_z(ra):
        k = (A - ra) % A
        if k < up_steps and (ra == 0 or ra > down_steps):
            ag_copy((ra, 0, 0), ((ra - 1) % A, 0, 0), dev(1, 0, 0))
        if ra < down_steps:
            ag_copy((ra, 0, 0), (ra + 1, 0, 0), dev(A - 1, 0, 0))

    to_z(0)
    to_y(0)
    to_core(0, 0)
    for load in loads[5:]:
        load.wait()

    order = [(0, 0)] + [(0, rb) for rb in range(1, B)] + [(ra, 0) for ra in zorder]
    order += [(ra, rb) for ra in zorder for rb in range(1, B)]

    def arrive(ra, rb):
        if (ra, rb) == (0, 0):
            return
        arrived(ag_slot(ra, rb, 0), ag_recv.at[sid(ra, rb, 0)])
        if rb == 0:
            to_z(ra)
            to_y(ra)
        to_core(ra, rb)

    def compute(ra, rb):
        i = cid(ra, rb)
        arrived(ag_slot(ra, rb, 1), ag_recv.at[sid(ra, rb, 1)])
        x = ag[i]
        gate = jnp.dot(x, wg_ref[...], preferred_element_type=jnp.float32)
        up = jnp.dot(x, wu_ref[...], preferred_element_type=jnp.float32)
        hidden = (gate / (1.0 + jnp.exp(-gate)) * up).astype(jnp.bfloat16)
        term = jnp.dot(hidden, wd_ref[...], preferred_element_type=jnp.float32)
        term = term.astype(jnp.bfloat16)
        own[i] = term[:R]
        core_st[i] = term[R:]
        send(core_st.at[i], core_land.at[i], core_send.at[i], core_recv.at[i], dev(0, 0, 1))

    def chip_sum(ra, rb):
        i = cid(ra, rb)
        arrived(core_land.at[i], core_recv.at[i])
        return own[i].astype(jnp.float32) + core_land[i].astype(jnp.float32)

    def y_step(ra, rb):
        i = cid(ra, rb)
        j = cid(ra, B - rb)
        y_st[i] = chip_sum(ra, rb).astype(jnp.bfloat16)
        send(y_st.at[i], y_land.at[j], y_send.at[i], y_recv.at[j], dev(0, rb, 0))

    def line_sum(ra):
        total = chip_sum(ra, 0)
        for rb in range(1, B):
            j = cid(ra, rb)
            arrived(y_land.at[j], y_recv.at[j])
            total = total + y_land[j].astype(jnp.float32)
        return total

    def z_step(ra):
        z_st[ra] = line_sum(ra).astype(jnp.bfloat16)
        send(z_st.at[ra], z_land.at[A - ra], z_send.at[ra], z_recv.at[A - ra], dev(ra, 0, 0))

    for k, pair in enumerate(order):
        if 0 < k and k + 1 < len(order):
            arrive(*order[k + 1])
        elif k == 0:
            pass
        compute(*pair)
        if k == 0:
            arrive(*order[1])
        if k >= 1 and order[k - 1][1]:
            y_step(*order[k - 1])
    if order[-1][1]:
        y_step(*order[-1])
    for ra in zorder:
        z_step(ra)
    total = line_sum(0)
    for ra in range(1, A):
        arrived(z_land.at[ra], z_recv.at[ra])
        total = total + z_land[ra].astype(jnp.float32)
    draft = x_ref[:R] + total
    x_ref[:R] = draft
    normed = rms_scale(draft, again_ref[...][None]).astype(bf16)
    q_ref[:R] = rotate(dot(normed, wq_ref[...]), cosp[:R], sinp[:R])
    kn_ref[:R] = rotate(dot(normed, wk_ref[...]), cosp[:R, :kw], sinp[:R, :kw])
    vn_ref[:R] = dot(normed, wv_ref[...]).astype(bf16)
    ctx = attend(q_ref[...], kc_ref[...], vc_ref[...], kn_ref[...], vn_ref[...], length)
    refined = x_ref[...] + dot(ctx, wo_ref[...])
    out_ref[...] = pick(move32.T.astype(bf16), refined)
    for copy in started:
        copy.wait_send()


def local(
    mesh_shape,
    tokens,
    cache_kv,
    cache_len,
    holder,
    accept,
    attn_gain,
    q_weight,
    k_weight,
    v_weight,
    o_weight,
    ffn_gain,
    w_gate,
    w_up,
    w_down,
):
    f32, bf16 = jnp.float32, jnp.bfloat16
    n, D = tokens.shape[1:]
    qw, kw = q_weight.shape[1], k_weight.shape[1]
    cs = cache_kv.shape[2]
    positions = (cache_len[0] + jnp.arange(n, dtype=jnp.int32)).astype(f32)
    lane = jnp.arange(qw, dtype=jnp.int32) % HEAD
    half = HEAD // 2
    freqs = jnp.exp(-jnp.log(rope_base) * 2.0 * (lane % half).astype(f32) / HEAD)
    angles = positions[:, None] * freqs[None, :]
    cosine = jnp.cos(angles)
    sine = jnp.where(lane < half, -1.0, 1.0) * jnp.sin(angles)
    R = ACCEPT
    A = 4
    B = mesh_shape["blk"] // (2 * A)
    G = mesh_shape["req"]
    pairs = A * B
    block = lambda m: pltpu.VMEM((m, R, D), bf16)
    dma = pltpu.SemaphoreType.DMA
    vmem = pl.BlockSpec(memory_space=pltpu.VMEM)
    smem = pl.BlockSpec(memory_space=pltpu.SMEM)
    anys = pl.BlockSpec(memory_space=pl.ANY)
    held = lambda w: pltpu.VMEM(w.shape, w.dtype)
    out = pl.pallas_call(
        functools.partial(layer_kernel, A, B, G),
        out_shape=jax.ShapeDtypeStruct((n, D), f32),
        in_specs=[smem] * 2 + [vmem] * 6 + [anys] * 8,
        out_specs=vmem,
        scratch_shapes=[
            held(q_weight), held(k_weight), held(v_weight), held(o_weight),
            held(w_gate), held(w_up), held(w_down),
            pltpu.VMEM((G, 2, cs, kw), bf16),
            pltpu.VMEM((cs, kw), bf16), pltpu.VMEM((cs, kw), bf16),
            pltpu.VMEM((n, qw), bf16), pltpu.VMEM((n, kw), bf16), pltpu.VMEM((n, kw), bf16),
            pltpu.VMEM((n, D), f32), pltpu.VMEM((n, qw), f32), pltpu.VMEM((n, qw), f32),
            dma((8,)), dma((G,)), dma((G,)),
            pltpu.VMEM((pairs, 2 * R, D), bf16),
            block(pairs), block(pairs), block(pairs), block(pairs), block(pairs),
            block(A), block(A),
            dma((2 * pairs,)), dma((2 * pairs,)),
            dma((pairs,)), dma((pairs,)), dma((pairs,)), dma((pairs,)),
            dma((A,)), dma((A,)),
        ],
        compiler_params=pltpu.CompilerParams(
            collective_id=0, has_side_effects=True, vmem_limit_bytes=58 * 2**20
        ),
    )(
        cache_len, holder, accept, tokens[0], cosine, sine, attn_gain, ffn_gain,
        cache_kv[0], q_weight, k_weight, v_weight, o_weight, w_gate, w_up, w_down,
    )
    return out[None]


def solution(mesh):
    return jax.shard_map(
        functools.partial(local, dict(mesh.shape)),
        mesh=mesh,
        in_specs=(
            P(("req", "blk"), None, None),
            P(("req", "blk"), None, None, None),
            P(("req", "blk")),
            P(("req", "blk")),
            P(("req", "blk"), None),
            P(),
            P(),
            P(),
            P(),
            P(),
            P(),
            P(None, "blk"),
            P(None, "blk"),
            P("blk", None),
        ),
        out_specs=P(("req", "blk"), None, None),
        check_vma=False,
    )
```
